128 devices in a mesh: yz: 32 (over z, y, core), sp: 4 (over x).
Axes of the slice: x: 4, y: 4, z: 4, core: 2. Of those that a mesh axis runs over, the one named last changes fastest.
Arguments:
- field: float32 [24, 256, 256, 256], P('sp', 'yz'), may hold values from -48 to 48
- start: float32 [256, 96], replicated, may hold values from -6 to 6
Outputs:
- core_block: float32 [24, 96, 256, 256], P('sp', None, 'yz')
- factor: float32 [256, 96], replicated
The draws below stay inside these ranges and needn't reach their ends.
All inputs are finite; a program needn't handle non-finite values.
Results may differ from the reference program's by a relative error of at most 0.00027.
Values sent between devices are 32-bit elements; how exact they have to be, the bound alone decides.
No kernel may reach another device: no remote copies, remote signals or barrier semaphores. Data moves between devices by JAX's collectives and lax.ppermute only.
A program may use at most 128 MiB of HBM per device.

```python
import math
import jax
import jax.numpy as jnp
from jax import lax

NX = 256
NS = 24
R = 96
NZ = 256
NY = 256


mode_count = 12


def draw_field(key, part):
    key = jax.random.fold_in(key, 7)
    subkeys = jax.random.split(key, 10)
    row_scale = jnp.exp(jax.random.uniform(subkeys[0], (1, NX, 1, 1), jnp.float32, 0.0, math.log(2.0)))
    cell_scale = jnp.exp(jax.random.uniform(subkeys[1], (1, NX, NY, 1), jnp.float32, 0.0, math.log(2.0)))
    species_scale = jnp.exp(jax.random.uniform(subkeys[2], (NS, 1, 1, 1), jnp.float32, 0.0, math.log(3.0)))
    rising = 1.0 + 2.0 * jnp.arange(NY, dtype=jnp.float32) / (NY - 1)
    rising = rising.reshape(1, 1, NY, 1)
    white_noise = jax.random.truncated_normal(subkeys[3], -4.0, 4.0, (NS, NX, NY, NZ), jnp.float32)
    along_x = white_noise + 0.45 * (jnp.roll(white_noise, 1, 1) + jnp.roll(white_noise, -1, 1))
    along_x = along_x + 0.2 * (jnp.roll(white_noise, 2, 1) + jnp.roll(white_noise, -2, 1))
    along_y = along_x + 0.5 * (jnp.roll(along_x, 1, 2) + jnp.roll(along_x, -1, 2))
    rough_part = along_y + 0.5 * (jnp.roll(along_y, 1, 3) + jnp.roll(along_y, -1, 3))
    rough_part = rough_part * (math.sqrt(0.95) / math.sqrt(1.485 * 1.5 * 1.5))
    profiles = jax.random.normal(subkeys[4], (mode_count, NX), jnp.float32)
    common = jax.random.normal(subkeys[5], (mode_count, 1), jnp.float32)
    own_part = jax.random.normal(subkeys[6], (mode_count, NS), jnp.float32)
    species_weights = 0.6 * common + 0.8 * own_part
    wave_y = jax.random.randint(subkeys[7], (mode_count,), 0, 4).astype(jnp.float32)
    wave_z = jax.random.randint(subkeys[8], (mode_count,), 0, 4).astype(jnp.float32)
    phases = jax.random.uniform(subkeys[9], (mode_count,), jnp.float32, -math.pi, math.pi)
    y_position = (jnp.arange(NY, dtype=jnp.float32) / NY).reshape(NY, 1)
    z_position = (jnp.arange(NZ, dtype=jnp.float32) / NZ).reshape(1, NZ)
    energies = [(1.0 + mode_index) ** (-5.0 / 3.0) for mode_index in range(mode_count)]
    energy_total = sum(energies)
    smooth_part = jnp.zeros((NS, NX, NY, NZ), jnp.float32)
    for mode_index in range(mode_count):
        amplitude = math.sqrt(2.0 * 0.05 * energies[mode_index] / energy_total)
        plane_wave = jnp.cos(2.0 * math.pi * (wave_y[mode_index] * y_position + wave_z[mode_index] * z_position) + phases[mode_index])
        smooth_part = smooth_part + amplitude * profiles[mode_index].reshape(1, NX, 1, 1) * species_weights[mode_index].reshape(NS, 1, 1, 1) * plane_wave.reshape(1, 1, NY, NZ)
    combined = (rough_part + smooth_part) * row_scale * cell_scale * species_scale * rising
    return jnp.clip(combined, -48.0, 48.0).astype(jnp.float32)


def centred(stream_key, extent, deviation, limit, kind=jnp.bfloat16):
    entries = jax.random.normal(stream_key, extent, jnp.float32) * deviation
    return jnp.minimum(jnp.maximum(entries, -limit), limit).astype(kind)


def setup_inputs(seed: int = 0) -> dict:
    key_of = jax.random.split(jax.random.key(seed), 3)
    return {
        "field": draw_field(jax.random.fold_in(key_of[2], 71), 0),
        "start": centred(key_of[1], (NX, R), 1.0, 6.0, jnp.float32),
    }


HIGH = lax.Precision.HIGHEST

def orth(matrix):
    square = jnp.dot(matrix.T, matrix, precision=HIGH)
    lower = jnp.linalg.cholesky(square)
    return lax.linalg.triangular_solve(lower, matrix, left_side=False, lower=True, transpose_a=True)

def reference(field, start):

    def accumulate(total, block):
        flat = block.reshape(block.shape[0], -1)
        return (total + jnp.dot(flat, flat.T, precision=HIGH), None)
    gram, unused = lax.scan(accumulate, jnp.zeros((NX, NX), jnp.float32), field)
    first = orth(jnp.dot(gram, start, precision=HIGH))
    factor = orth(jnp.dot(gram, first, precision=HIGH))

    def project(block):
        return jnp.einsum('xr,xyz->ryz', factor, block, precision=HIGH)
    core_block = lax.map(project, field)
    return (core_block, factor)
```

```python
import jax
import jax.numpy as jnp
from jax import lax
from jax.experimental import pallas as pl
from jax.experimental.pallas import tpu as pltpu
from jax.sharding import PartitionSpec as P

HIGH = lax.Precision.HIGHEST
F32 = jnp.float32
BF16 = jnp.bfloat16
VMEM_BYTES = 56 << 20
ROWS_BY_ROWS = (((1,), (1,)), ((), ()))


def split(value):
    high = value.astype(BF16)
    low = (value - high.astype(F32)).astype(BF16)
    return high, low


def pack(field, rows):
    ns, nx, ny, nz = field.shape
    depth = 64

    def kernel(in_ref, out_ref):
        for block in range(depth // rows):
            out_ref[block, 0] = jnp.swapaxes(in_ref[0, :, block * rows : (block + 1) * rows, :], 0, 1)

    return pl.pallas_call(
        kernel,
        grid=(ny // depth, ns),
        out_shape=jax.ShapeDtypeStruct((ny // rows, ns, rows, nx, nz), F32),
        in_specs=[pl.BlockSpec((1, nx, depth, nz), lambda y, s: (s, 0, y, 0))],
        out_specs=pl.BlockSpec((depth // rows, 1, rows, nx, nz), lambda y, s: (y, s, 0, 0, 0)),
        compiler_params=pltpu.CompilerParams(vmem_limit_bytes=VMEM_BYTES),
        name="pack",
    )(field)


def gram(fibres):
    nb, ns, ny, nx, nz = fibres.shape
    order = nb * nx

    def kernel(in_ref, out_ref, total):
        step = pl.program_id(0)
        parts = [split(in_ref[:, 0, y].reshape(order, nz)) for y in range(ny)]
        high = jnp.concatenate([part[0] for part in parts], axis=1)
        low = jnp.concatenate([part[1] for part in parts], axis=1)
        square = lax.dot_general(high, high, ROWS_BY_ROWS, preferred_element_type=F32)
        cross = lax.dot_general(high, low, ROWS_BY_ROWS, preferred_element_type=F32)

        @pl.when(step == 0)
        def _():
            total[0] = square
            total[1] = cross

        @pl.when(step > 0)
        def _():
            total[0] += square
            total[1] += cross

        @pl.when(step == ns - 1)
        def _():
            out_ref[...] = total[0] + (total[1] + total[1].T)

    return pl.pallas_call(
        kernel,
        grid=(ns,),
        out_shape=jax.ShapeDtypeStruct((order, order), F32),
        in_specs=[pl.BlockSpec((nb, 1, ny, nx, nz), lambda s: (0, s, 0, 0, 0))],
        out_specs=pl.BlockSpec((order, order), lambda s: (0, 0)),
        scratch_shapes=[pltpu.VMEM((2, order, order), F32)],
        compiler_params=pltpu.CompilerParams(vmem_limit_bytes=VMEM_BYTES),
        name="gram",
    )(fibres)


def sum_everywhere(partial):
    n, m = partial.shape
    nb = lax.axis_size("yz")
    np_ = lax.axis_size("sp")
    rows = lax.all_to_all(partial.reshape(nb, n // nb, m), "yz", 0, 0, tiled=True)
    rows = jnp.sum(rows, axis=0)
    near, across, far = [
        lax.ppermute(rows, "sp", [(i, (i + step) % np_) for i in range(np_)])
        for step in range(1, np_)
    ]
    rows = (rows + across) + (near + far)
    copies = jnp.broadcast_to(rows[None], (nb, n // nb, m))
    return lax.all_to_all(copies, "yz", 0, 0, tiled=True).reshape(n, m)


def orth_rows(rows, count):
    square = lax.dot_general(rows, rows, ROWS_BY_ROWS, precision=HIGH, preferred_element_type=F32)
    index = lax.broadcasted_iota(jnp.int32, (count, 1), 0)
    for j in range(count):
        pivot_row = square[j : j + 1, :]
        data_row = rows[j : j + 1, :]
        scale = lax.rsqrt(square[j : j + 1, j : j + 1])
        column = jnp.where(index > j, square[:, j : j + 1] * (scale * scale), 0.0)
        square = square - column * pivot_row
        rows = rows - column * data_row
        rows = jnp.where(index == j, data_row * scale, rows)
    return rows


def iterate(gram_matrix, start_rows):
    count, order = start_rows.shape

    def kernel(gram_ref, start_ref, out_ref):
        whole = gram_ref[...]
        rows = jnp.dot(start_ref[...], whole, precision=HIGH, preferred_element_type=F32)
        rows = orth_rows(rows, count)
        rows = jnp.dot(rows, whole, precision=HIGH, preferred_element_type=F32)
        out_ref[...] = orth_rows(rows, count)

    return pl.pallas_call(
        kernel,
        out_shape=jax.ShapeDtypeStruct((count, order), F32),
        compiler_params=pltpu.CompilerParams(vmem_limit_bytes=VMEM_BYTES),
        name="iterate",
    )(gram_matrix, start_rows)


def project(fibres, factor_rows):
    nb, ns, ny, nx, nz = fibres.shape
    order = nb * nx
    count = factor_rows.shape[0]

    def kernel(in_ref, factor_ref, out_ref):
        high_rows, low_rows = split(factor_ref[...])
        both = jnp.concatenate([high_rows, low_rows], axis=0)
        for y in range(ny):
            high, low = split(in_ref[:, 0, y].reshape(order, nz))
            first = jnp.dot(both, high, preferred_element_type=F32)
            second = jnp.dot(high_rows, low, preferred_element_type=F32)
            out_ref[:, y, :] = first[:count] + (first[count:] + second)

    return pl.pallas_call(
        kernel,
        grid=(ns,),
        out_shape=jax.ShapeDtypeStruct((ns, count, ny, nz), F32),
        in_specs=[
            pl.BlockSpec((nb, 1, ny, nx, nz), lambda s: (0, s, 0, 0, 0)),
            pl.BlockSpec((count, order), lambda s: (0, 0)),
        ],
        out_specs=pl.BlockSpec((None, count, ny, nz), lambda s: (s, 0, 0, 0)),
        compiler_params=pltpu.CompilerParams(vmem_limit_bytes=VMEM_BYTES),
        name="project",
    )(fibres, factor_rows)


def local(field, start):
    nb = lax.axis_size("yz")
    blocks = pack(field, field.shape[2] // nb)
    fibres = lax.all_to_all(blocks, "yz", split_axis=0, concat_axis=0, tiled=True)
    total = sum_everywhere(gram(fibres))
    factor_rows = iterate(total, start.T)
    core_block = project(fibres, factor_rows)
    return (core_block, factor_rows.T)


def solution(mesh):
    in_specs = (P("sp", "yz", None, None), P())
    out_specs = (P("sp", None, "yz", None), P())
    return jax.shard_map(local, mesh=mesh, in_specs=in_specs, out_specs=out_specs, check_vma=False)
```

```python
import jax
import jax.numpy as jnp
from jax import lax
from jax.experimental import pallas as pl
from jax.experimental.pallas import tpu as pltpu
from jax.sharding import PartitionSpec as P

HIGH = lax.Precision.HIGHEST
F32 = jnp.float32
BF16 = jnp.bfloat16
LANES = 128
ROWS_BY_ROWS = (((1,), (1,)), ((), ()))


def split(value):
    high = value.astype(BF16)
    low = (value - high.astype(F32)).astype(BF16)
    return high, low


def pack(field, rows):
    ns, nx, ny, nz = field.shape
    depth = 256

    def kernel(in_ref, out_ref):
        for block in range(depth // rows):
            out_ref[block, 0] = jnp.swapaxes(in_ref[0, :, block * rows : (block + 1) * rows, :], 0, 1)

    return pl.pallas_call(
        kernel,
        grid=(ny // depth, ns),
        out_shape=jax.ShapeDtypeStruct((ny // rows, ns, rows, nx, nz), F32),
        in_specs=[pl.BlockSpec((1, nx, depth, nz), lambda y, s: (s, 0, y, 0))],
        out_specs=pl.BlockSpec((depth // rows, 1, rows, nx, nz), lambda y, s: (y, s, 0, 0, 0)),
        compiler_params=pltpu.CompilerParams(vmem_limit_bytes=40 << 20),
        name="pack",
    )(field)


def gram(fibres):
    nb, ns, ny, nx, nz = fibres.shape
    order = nb * nx

    def kernel(in_ref, out_ref, terms_ref, total):
        step = pl.program_id(0)
        highs, lows = [], []
        for y in range(ny):
            high, low = split(in_ref[:, 0, y].reshape(order, nz))
            terms_ref[0, 0, y] = high
            terms_ref[1, 0, y] = low
            highs.append(high)
            lows.append(low)
        high = jnp.concatenate(highs, axis=1)
        low = jnp.concatenate(lows, axis=1)
        square = lax.dot_general(high, high, ROWS_BY_ROWS, preferred_element_type=F32)
        cross = lax.dot_general(high, low, ROWS_BY_ROWS, preferred_element_type=F32)

        @pl.when(step == 0)
        def _():
            total[0] = square
            total[1] = cross

        @pl.when(step > 0)
        def _():
            total[0] += square
            total[1] += cross

        @pl.when(step == ns - 1)
        def _():
            out_ref[...] = total[0] + (total[1] + total[1].T)

    return pl.pallas_call(
        kernel,
        grid=(ns,),
        out_shape=(
            jax.ShapeDtypeStruct((order, order), F32),
            pltpu.HBM((2, ns, ny, order, nz), BF16),
        ),
        in_specs=[pl.BlockSpec((nb, 1, ny, nx, nz), lambda s: (0, s, 0, 0, 0))],
        out_specs=(
            pl.BlockSpec((order, order), lambda s: (0, 0)),
            pl.BlockSpec((2, 1, ny, order, nz), lambda s: (0, s, 0, 0, 0)),
        ),
        scratch_shapes=[pltpu.VMEM((2, order, order), F32)],
        compiler_params=pltpu.CompilerParams(vmem_limit_bytes=24 << 20),
        name="gram",
    )(fibres)


def sum_everywhere(partial):
    n, m = partial.shape
    nb = lax.axis_size("yz")
    np_ = lax.axis_size("sp")
    rows = lax.all_to_all(partial.reshape(nb, n // nb, m), "yz", 0, 0, tiled=True)
    rows = jnp.sum(rows, axis=0)
    near, across, far = [
        lax.ppermute(rows, "sp", [(i, (i + step) % np_) for i in range(np_)])
        for step in range(1, np_)
    ]
    rows = (rows + across) + (near + far)
    copies = jnp.broadcast_to(rows[None], (nb, n // nb, m))
    return lax.all_to_all(copies, "yz", 0, 0, tiled=True).reshape(n, m)


def eliminate(square, rows, put, size=8):
    count, width = rows.shape
    halves = width // LANES
    spread = lambda value: jnp.broadcast_to(value, (size, LANES))
    left = [
        [square[t : t + size]] + [rows[t : t + size, h * LANES : (h + 1) * LANES] for h in range(halves)]
        for t in range(0, count, size)
    ]
    for block in range(count // size):
        first = block * size
        rest = range(block + 1, count // size)
        pivots = [[spread(part[i : i + 1]) for part in left[block]] for i in range(size)]
        entry = [
            [spread(pivots[i][0][:, first + j : first + j + 1]) for j in range(i + 1)] for i in range(size)
        ]
        columns = [{t: spread(left[t][0][:, first + j : first + j + 1]) for t in rest} for j in range(size)]
        factor = [[None] * size for _ in range(size)]
        inverse = [None] * size
        for j in range(size):
            inverse[j] = 1.0 / entry[j][j]
            for i in range(j + 1, size):
                factor[i][j] = entry[i][j] * inverse[j]
            for i in range(j + 1, size):
                for m in range(j + 1, i + 1):
                    entry[i][m] = entry[i][m] - factor[i][j] * entry[m][j]
        for i in range(size):
            for j in range(i):
                pivots[i] = [a - factor[i][j] * b for a, b in zip(pivots[i], pivots[j])]
                for t in rest:
                    columns[i][t] = columns[i][t] - factor[i][j] * columns[j][t]
            scale = lax.rsqrt(entry[i][i])
            for h in range(halves):
                put(first + i, h, (pivots[i][1 + h] * scale)[0:1])
        for t in rest:
            for i in range(size):
                multiple = columns[i][t] * inverse[i]
                left[t] = [a - multiple * b for a, b in zip(left[t], pivots[i])]


def finish(gram_matrix, start_rows, terms):
    count, order = start_rows.shape
    _, ns, ny, _, nz = terms.shape

    def kernel(gram_ref, start_ref, terms_ref, core_ref, factor_ref, held, made, in_sems, out_sems):
        def arrival(s):
            return pltpu.make_async_copy(terms_ref.at[:, s], held.at[:, s], in_sems.at[s])

        def leaving(s):
            return pltpu.make_async_copy(made.at[s], core_ref.at[s], out_sems.at[s])

        for s in range(ns):
            arrival(s).start()

        def orth(rows, out_ref):
            rows = rows * lax.rsqrt(jnp.sum(rows * rows, axis=1, keepdims=True))
            square = lax.dot_general(rows, rows, ROWS_BY_ROWS, precision=HIGH, preferred_element_type=F32)
            square = jnp.concatenate([square, jnp.zeros((count, LANES - count), F32)], axis=1)

            def put(i, h, value):
                out_ref[i : i + 1, h * LANES : (h + 1) * LANES] = value

            eliminate(square, rows, put)

        whole = gram_ref[...]
        factor_ref[...] = start_ref[...]

        def step(index, carry):
            orth(jnp.dot(factor_ref[...], whole, precision=HIGH, preferred_element_type=F32), factor_ref)
            return carry

        lax.fori_loop(0, 2, step, 0)

        high_rows, low_rows = split(factor_ref[...])
        both = jnp.concatenate([high_rows, low_rows], axis=0)

        def species(s, carry):
            arrival(s).wait()
            results = []
            for y in range(ny):
                main = jnp.dot(both, held[0, s, y], preferred_element_type=F32)
                more = jnp.dot(high_rows, held[1, s, y], preferred_element_type=F32)
                results.append(main[:count] + (main[count:] + more))
            made[s] = jnp.swapaxes(jnp.stack(results), 0, 1)
            leaving(s).start()
            return carry

        lax.fori_loop(0, ns, species, 0)
        for s in range(ns):
            leaving(s).wait()

    whole_vmem = pl.BlockSpec(memory_space=pltpu.VMEM)
    anywhere = pl.BlockSpec(memory_space=pl.ANY)
    return pl.pallas_call(
        kernel,
        out_shape=(
            jax.ShapeDtypeStruct((ns, count, ny, nz), F32),
            jax.ShapeDtypeStruct((count, order), F32),
        ),
        in_specs=[whole_vmem, whole_vmem, anywhere],
        out_specs=(anywhere, whole_vmem),
        scratch_shapes=[
            pltpu.VMEM((2, ns, ny, order, nz), BF16),
            pltpu.VMEM((ns, count, ny, nz), F32),
            pltpu.SemaphoreType.DMA((ns,)),
            pltpu.SemaphoreType.DMA((ns,)),
        ],
        compiler_params=pltpu.CompilerParams(vmem_limit_bytes=56 << 20),
        name="finish",
    )(gram_matrix, start_rows, terms)


def local(field, start):
    nb = lax.axis_size("yz")
    blocks = pack(field, field.shape[2] // nb)
    fibres = lax.all_to_all(blocks, "yz", split_axis=0, concat_axis=0, tiled=True)
    partial, terms = gram(fibres)
    total = sum_everywhere(partial)
    core_block, factor_rows = finish(total, start.T, terms)
    return (core_block, factor_rows.T)


def solution(mesh):
    in_specs = (P("sp", "yz", None, None), P())
    out_specs = (P("sp", None, "yz", None), P())
    return jax.shard_map(local, mesh=mesh, in_specs=in_specs, out_specs=out_specs, check_vma=False)
```

```python
import jax
import jax.numpy as jnp
from jax import lax
from jax.experimental import pallas as pl
from jax.experimental.pallas import tpu as pltpu
from jax.sharding import PartitionSpec as P

HIGH = lax.Precision.HIGHEST
F32 = jnp.float32
BF16 = jnp.bfloat16
LANES = 128
ROWS_BY_ROWS = (((1,), (1,)), ((), ()))


def split(value):
    high = value.astype(BF16)
    low = (value - high.astype(F32)).astype(BF16)
    return high, low


def pack(field, rows):
    ns, nx, ny, nz = field.shape

    def kernel(in_ref, out_ref, held, in_sems):
        def arrival(s):
            return pltpu.make_async_copy(in_ref.at[s], held.at[s], in_sems.at[s])

        for s in range(ns):
            arrival(s).start()

        def species(s, carry):
            arrival(s).wait()

            for block in range(ny // rows):
                out_ref[block, s] = jnp.swapaxes(held[s, :, block * rows : (block + 1) * rows, :], 0, 1)
            return carry

        lax.fori_loop(0, ns, species, 0)

    return pl.pallas_call(
        kernel,
        out_shape=pltpu.VMEM((ny // rows, ns, rows, nx, nz), F32),
        in_specs=[pl.BlockSpec(memory_space=pl.ANY)],
        out_specs=pl.BlockSpec(memory_space=pltpu.VMEM),
        scratch_shapes=[
            pltpu.VMEM((ns, nx, ny, nz), F32),
            pltpu.SemaphoreType.DMA((ns,)),
        ],
        compiler_params=pltpu.CompilerParams(vmem_limit_bytes=40 << 20),
        name="pack",
    )(field)


def gram(fibres):
    nb, ns, ny, nx, nz = fibres.shape
    order = nb * nx

    def kernel(in_ref, out_ref, terms_ref, held, total, sems):
        def leaving(s):
            return pltpu.make_async_copy(held.at[:, s], terms_ref.at[:, s], sems.at[s])

        total[...] = jnp.zeros_like(total)

        def halve(s):
            for y in range(ny):
                held[0, s, y], held[1, s, y] = split(in_ref[:, s, y].reshape(order, nz))
            leaving(s).start()

        halve(0)
        for s in range(ns):
            if s + 1 < ns:
                halve(s + 1)
            high = jnp.concatenate([held[0, s, y] for y in range(ny)], axis=1)
            low = jnp.concatenate([held[1, s, y] for y in range(ny)], axis=1)
            total[0] += lax.dot_general(high, high, ROWS_BY_ROWS, preferred_element_type=F32)
            total[1] += lax.dot_general(high, low, ROWS_BY_ROWS, preferred_element_type=F32)
        out_ref[...] = total[0] + (total[1] + total[1].T)
        for s in range(ns):
            leaving(s).wait()

    return pl.pallas_call(
        kernel,
        out_shape=(
            jax.ShapeDtypeStruct((order, order), F32),
            pltpu.HBM((2, ns, ny, order, nz), BF16),
        ),
        in_specs=[pl.BlockSpec(memory_space=pltpu.VMEM)],
        out_specs=(pl.BlockSpec(memory_space=pltpu.VMEM), pl.BlockSpec(memory_space=pl.ANY)),
        scratch_shapes=[
            pltpu.VMEM((2, ns, ny, order, nz), BF16),
            pltpu.VMEM((2, order, order), F32),
            pltpu.SemaphoreType.DMA((ns,)),
        ],
        compiler_params=pltpu.CompilerParams(vmem_limit_bytes=30 << 20),
        name="gram",
    )(fibres)


def sum_everywhere(partial):
    n, m = partial.shape
    nb = lax.axis_size("yz")
    np_ = lax.axis_size("sp")
    rows = lax.all_to_all(partial.reshape(nb, n // nb, m), "yz", 0, 0, tiled=True)
    rows = jnp.sum(rows, axis=0)
    near, across, far = [
        lax.ppermute(rows, "sp", [(i, (i + step) % np_) for i in range(np_)])
        for step in range(1, np_)
    ]
    rows = (rows + across) + (near + far)
    copies = jnp.broadcast_to(rows[None], (nb, n // nb, m))
    return lax.all_to_all(copies, "yz", 0, 0, tiled=True).reshape(n, m)


def eliminate(square, rows, put, size=8):
    count, width = rows.shape
    halves = width // LANES
    spread = lambda value: jnp.broadcast_to(value, (size, LANES))
    left = [
        [square[t : t + size]] + [rows[t : t + size, h * LANES : (h + 1) * LANES] for h in range(halves)]
        for t in range(0, count, size)
    ]
    for block in range(count // size):
        first = block * size
        rest = range(block + 1, count // size)
        pivots = [[spread(part[i : i + 1]) for part in left[block]] for i in range(size)]
        entry = [
            [spread(pivots[i][0][:, first + j : first + j + 1]) for j in range(i + 1)] for i in range(size)
        ]
        columns = [{t: spread(left[t][0][:, first + j : first + j + 1]) for t in rest} for j in range(size)]
        factor = [[None] * size for _ in range(size)]
        inverse = [None] * size
        for j in range(size):
            inverse[j] = 1.0 / entry[j][j]
            for i in range(j + 1, size):
                factor[i][j] = entry[i][j] * inverse[j]
            for i in range(j + 1, size):
                for m in range(j + 1, i + 1):
                    entry[i][m] = entry[i][m] - factor[i][j] * entry[m][j]
        for i in range(size):
            for j in range(i):
                pivots[i] = [a - factor[i][j] * b for a, b in zip(pivots[i], pivots[j])]
                for t in rest:
                    columns[i][t] = columns[i][t] - factor[i][j] * columns[j][t]
            scale = lax.rsqrt(entry[i][i])
            for h in range(halves):
                put(first + i, h, (pivots[i][1 + h] * scale)[0:1])
        for t in rest:
            for i in range(size):
                multiple = columns[i][t] * inverse[i]
                left[t] = [a - multiple * b for a, b in zip(left[t], pivots[i])]


def finish(gram_matrix, start_rows, terms):
    count, order = start_rows.shape
    _, ns, ny, _, nz = terms.shape

    def kernel(gram_ref, start_ref, terms_ref, core_ref, factor_ref, held, made, in_sems, out_sems):
        def arrival(s):
            return pltpu.make_async_copy(terms_ref.at[:, s], held.at[:, s], in_sems.at[s])

        def leaving(s):
            return pltpu.make_async_copy(made.at[s], core_ref.at[s], out_sems.at[s])

        for s in range(ns):
            arrival(s).start()

        def orth(rows, out_ref):
            rows = rows * lax.rsqrt(jnp.sum(rows * rows, axis=1, keepdims=True))
            square = lax.dot_general(rows, rows, ROWS_BY_ROWS, precision=HIGH, preferred_element_type=F32)
            square = jnp.concatenate([square, jnp.zeros((count, LANES - count), F32)], axis=1)

            def put(i, h, value):
                out_ref[i : i + 1, h * LANES : (h + 1) * LANES] = value

            eliminate(square, rows, put)

        whole = gram_ref[...]
        factor_ref[...] = start_ref[...]

        def step(index, carry):
            orth(jnp.dot(factor_ref[...], whole, precision=HIGH, preferred_element_type=F32), factor_ref)
            return carry

        lax.fori_loop(0, 2, step, 0)

        high_rows, low_rows = split(factor_ref[...])
        both = jnp.concatenate([high_rows, low_rows], axis=0)

        def species(s, carry):
            arrival(s).wait()
            results = []
            for y in range(ny):
                main = jnp.dot(both, held[0, s, y], preferred_element_type=F32)
                more = jnp.dot(high_rows, held[1, s, y], preferred_element_type=F32)
                results.append(main[:count] + (main[count:] + more))
            made[s] = jnp.swapaxes(jnp.stack(results), 0, 1)
            leaving(s).start()
            return carry

        lax.fori_loop(0, ns, species, 0)
        for s in range(ns):
            leaving(s).wait()

    whole_vmem = pl.BlockSpec(memory_space=pltpu.VMEM)
    anywhere = pl.BlockSpec(memory_space=pl.ANY)
    return pl.pallas_call(
        kernel,
        out_shape=(
            jax.ShapeDtypeStruct((ns, count, ny, nz), F32),
            jax.ShapeDtypeStruct((count, order), F32),
        ),
        in_specs=[whole_vmem, whole_vmem, anywhere],
        out_specs=(anywhere, whole_vmem),
        scratch_shapes=[
            pltpu.VMEM((2, ns, ny, order, nz), BF16),
            pltpu.VMEM((ns, count, ny, nz), F32),
            pltpu.SemaphoreType.DMA((ns,)),
            pltpu.SemaphoreType.DMA((ns,)),
        ],
        compiler_params=pltpu.CompilerParams(vmem_limit_bytes=56 << 20),
        name="finish",
    )(gram_matrix, start_rows, terms)


def local(field, start):
    nb = lax.axis_size("yz")
    blocks = pack(field, field.shape[2] // nb)
    fibres = lax.all_to_all(blocks, "yz", split_axis=0, concat_axis=0, tiled=True)
    partial, terms = gram(fibres)
    total = sum_everywhere(partial)
    core_block, factor_rows = finish(total, start.T, terms)
    return (core_block, factor_rows.T)


def solution(mesh):
    in_specs = (P("sp", "yz", None, None), P())
    out_specs = (P("sp", None, "yz", None), P())
    return jax.shard_map(local, mesh=mesh, in_specs=in_specs, out_specs=out_specs, check_vma=False)
```

```python
import jax
import jax.numpy as jnp
from jax import lax
from jax.experimental import pallas as pl
from jax.experimental.pallas import tpu as pltpu
from jax.sharding import PartitionSpec as P

HIGH = lax.Precision.HIGHEST
F32 = jnp.float32
BF16 = jnp.bfloat16
LANES = 128
ROWS_BY_ROWS = (((1,), (1,)), ((), ()))


def split(value):
    high = value.astype(BF16)
    low = (value - high.astype(F32)).astype(BF16)
    return high, low


def pack(field, rows):
    ns, nx, ny, nz = field.shape

    def kernel(in_ref, out_ref, held, in_sems):
        def arrival(s):
            return pltpu.make_async_copy(in_ref.at[s], held.at[s], in_sems.at[s])

        for s in range(ns):
            arrival(s).start()

        def species(s, carry):
            arrival(s).wait()

            for block in range(ny // rows):
                out_ref[block, s] = jnp.swapaxes(held[s, :, block * rows : (block + 1) * rows, :], 0, 1)
            return carry

        lax.fori_loop(0, ns, species, 0)

    return pl.pallas_call(
        kernel,
        out_shape=pltpu.VMEM((ny // rows, ns, rows, nx, nz), F32),
        in_specs=[pl.BlockSpec(memory_space=pl.ANY)],
        out_specs=pl.BlockSpec(memory_space=pltpu.VMEM),
        scratch_shapes=[
            pltpu.VMEM((ns, nx, ny, nz), F32),
            pltpu.SemaphoreType.DMA((ns,)),
        ],
        compiler_params=pltpu.CompilerParams(vmem_limit_bytes=40 << 20),
        name="pack",
    )(field)


def gram(fibres):
    nb, ns, ny, nx, nz = fibres.shape
    order = nb * nx

    def kernel(in_ref, out_ref, terms_ref, held, total, sems):
        def leaving(s):
            return pltpu.make_async_copy(held.at[:, s], terms_ref.at[:, s], sems.at[s])

        total[...] = jnp.zeros_like(total)

        def halve(s):
            for y in range(ny):
                held[0, s, y], held[1, s, y] = split(in_ref[:, s, y].reshape(order, nz))
            leaving(s).start()

        halve(0)
        for s in range(ns):
            if s + 1 < ns:
                halve(s + 1)
            high = jnp.concatenate([held[0, s, y] for y in range(ny)], axis=1)
            low = jnp.concatenate([held[1, s, y] for y in range(ny)], axis=1)
            total[0] += lax.dot_general(high, high, ROWS_BY_ROWS, preferred_element_type=F32)
            total[1] += lax.dot_general(high, low, ROWS_BY_ROWS, preferred_element_type=F32)
        whole = total[0] + (total[1] + total[1].T)
        for h in range(order // LANES):
            out_ref[h * order : (h + 1) * order] = whole[:, h * LANES : (h + 1) * LANES]
        for s in range(ns):
            leaving(s).wait()

    return pl.pallas_call(
        kernel,
        out_shape=(
            jax.ShapeDtypeStruct((order * (order // LANES), LANES), F32),
            pltpu.HBM((2, ns, ny, order, nz), BF16),
        ),
        in_specs=[pl.BlockSpec(memory_space=pltpu.VMEM)],
        out_specs=(pl.BlockSpec(memory_space=pltpu.VMEM), pl.BlockSpec(memory_space=pl.ANY)),
        scratch_shapes=[
            pltpu.VMEM((2, ns, ny, order, nz), BF16),
            pltpu.VMEM((2, order, order), F32),
            pltpu.SemaphoreType.DMA((ns,)),
        ],
        compiler_params=pltpu.CompilerParams(vmem_limit_bytes=30 << 20),
        name="gram",
    )(fibres)


def sum_everywhere(partial):
    n, m = partial.shape
    everyone = ("yz", "sp")
    size = lax.axis_size("yz") * lax.axis_size("sp")
    parts = lax.all_to_all(partial.reshape(size, n // size, m), everyone, 0, 0, tiled=True)
    copies = jnp.broadcast_to(jnp.sum(parts, axis=0)[None], parts.shape)
    return lax.all_to_all(copies, everyone, 0, 0, tiled=True).reshape(n, m)


def eliminate(square, rows, put, size=8):
    count, width = rows.shape
    halves = width // LANES
    spread = lambda value: jnp.broadcast_to(value, (size, LANES))
    left = [
        [square[t : t + size]] + [rows[t : t + size, h * LANES : (h + 1) * LANES] for h in range(halves)]
        for t in range(0, count, size)
    ]
    for block in range(count // size):
        first = block * size
        rest = range(block + 1, count // size)
        pivots = [[spread(part[i : i + 1]) for part in left[block]] for i in range(size)]
        entry = [
            [spread(pivots[i][0][:, first + j : first + j + 1]) for j in range(i + 1)] for i in range(size)
        ]
        columns = [{t: spread(left[t][0][:, first + j : first + j + 1]) for t in rest} for j in range(size)]
        factor = [[None] * size for _ in range(size)]
        inverse = [None] * size
        for j in range(size):
            inverse[j] = 1.0 / entry[j][j]
            for i in range(j + 1, size):
                factor[i][j] = entry[i][j] * inverse[j]
            for i in range(j + 1, size):
                for m in range(j + 1, i + 1):
                    entry[i][m] = entry[i][m] - factor[i][j] * entry[m][j]
        for i in range(size):
            for j in range(i):
                pivots[i] = [a - factor[i][j] * b for a, b in zip(pivots[i], pivots[j])]
                for t in rest:
                    columns[i][t] = columns[i][t] - factor[i][j] * columns[j][t]
            scale = lax.rsqrt(entry[i][i])
            for h in range(halves):
                put(first + i, h, (pivots[i][1 + h] * scale)[0:1])
        for t in rest:
            for i in range(size):
                multiple = columns[i][t] * inverse[i]
                left[t] = [a - multiple * b for a, b in zip(left[t], pivots[i])]


def finish(gram_matrix, start_rows, terms):
    count, order = start_rows.shape
    _, ns, ny, _, nz = terms.shape

    def kernel(gram_ref, start_ref, terms_ref, core_ref, factor_ref, held, made, in_sems, out_sems):
        def arrival(s):
            return pltpu.make_async_copy(terms_ref.at[:, s], held.at[:, s], in_sems.at[s])

        def leaving(s):
            return pltpu.make_async_copy(made.at[s], core_ref.at[s], out_sems.at[s])

        for s in range(ns):
            arrival(s).start()

        def orth(rows, out_ref):
            rows = rows * lax.rsqrt(jnp.sum(rows * rows, axis=1, keepdims=True))
            square = lax.dot_general(rows, rows, ROWS_BY_ROWS, precision=HIGH, preferred_element_type=F32)
            square = jnp.concatenate([square, jnp.zeros((count, LANES - count), F32)], axis=1)

            def put(i, h, value):
                out_ref[i : i + 1, h * LANES : (h + 1) * LANES] = value

            eliminate(square, rows, put)

        whole = jnp.concatenate([gram_ref[h * order : (h + 1) * order] for h in range(order // LANES)], axis=1)
        factor_ref[...] = start_ref[...]

        def step(index, carry):
            orth(jnp.dot(factor_ref[...], whole, precision=HIGH, preferred_element_type=F32), factor_ref)
            return carry

        lax.fori_loop(0, 2, step, 0)

        high_rows, low_rows = split(factor_ref[...])
        both = jnp.concatenate([high_rows, low_rows], axis=0)

        def species(s, carry):
            arrival(s).wait()
            results = []
            for y in range(ny):
                main = jnp.dot(both, held[0, s, y], preferred_element_type=F32)
                more = jnp.dot(high_rows, held[1, s, y], preferred_element_type=F32)
                results.append(main[:count] + (main[count:] + more))
            made[s] = jnp.swapaxes(jnp.stack(results), 0, 1)
            leaving(s).start()
            return carry

        lax.fori_loop(0, ns, species, 0)
        for s in range(ns):
            leaving(s).wait()

    whole_vmem = pl.BlockSpec(memory_space=pltpu.VMEM)
    anywhere = pl.BlockSpec(memory_space=pl.ANY)
    return pl.pallas_call(
        kernel,
        out_shape=(
            jax.ShapeDtypeStruct((ns, count, ny, nz), F32),
            jax.ShapeDtypeStruct((count, order), F32),
        ),
        in_specs=[whole_vmem, whole_vmem, anywhere],
        out_specs=(anywhere, whole_vmem),
        scratch_shapes=[
            pltpu.VMEM((2, ns, ny, order, nz), BF16),
            pltpu.VMEM((ns, count, ny, nz), F32),
            pltpu.SemaphoreType.DMA((ns,)),
            pltpu.SemaphoreType.DMA((ns,)),
        ],
        compiler_params=pltpu.CompilerParams(vmem_limit_bytes=56 << 20),
        name="finish",
    )(gram_matrix, start_rows, terms)


def local(field, start):
    nb = lax.axis_size("yz")
    blocks = pack(field, field.shape[2] // nb)
    fibres = lax.all_to_all(blocks, "yz", split_axis=0, concat_axis=0, tiled=True)
    partial, terms = gram(fibres)
    total = sum_everywhere(partial)
    core_block, factor_rows = finish(total, start.T, terms)
    return (core_block, factor_rows.T)


def solution(mesh):
    in_specs = (P("sp", "yz", None, None), P())
    out_specs = (P("sp", None, "yz", None), P())
    return jax.shard_map(local, mesh=mesh, in_specs=in_specs, out_specs=out_specs, check_vma=False)
```

```python
import jax
import jax.numpy as jnp
from jax import lax
from jax.experimental import pallas as pl
from jax.experimental.pallas import tpu as pltpu
from jax.sharding import PartitionSpec as P

HIGH = lax.Precision.HIGHEST
F32 = jnp.float32
BF16 = jnp.bfloat16
LANES = 128
ROWS_BY_ROWS = (((1,), (1,)), ((), ()))


def split(value):
    high = value.astype(BF16)
    low = (value - high.astype(F32)).astype(BF16)
    return high, low


def pack(field, rows):
    ns, nx, ny, nz = field.shape

    parts = 4
    depth = ny // parts

    def kernel(in_ref, out_ref, held, in_sems):
        def arrival(s, part):
            some = pl.ds(part * depth, depth)
            return pltpu.make_async_copy(in_ref.at[s, :, some], held.at[s, :, some], in_sems.at[s, part])

        for s in range(ns):
            for part in range(parts):
                arrival(s, part).start()

        def species(s, carry):
            for part in range(parts):
                arrival(s, part).wait()
                for block in range(part * depth // rows, (part + 1) * depth // rows):
                    out_ref[block, s] = jnp.swapaxes(held[s, :, block * rows : (block + 1) * rows, :], 0, 1)
            return carry

        lax.fori_loop(0, ns, species, 0)

    return pl.pallas_call(
        kernel,
        out_shape=pltpu.VMEM((ny // rows, ns, rows, nx, nz), F32),
        in_specs=[pl.BlockSpec(memory_space=pl.ANY)],
        out_specs=pl.BlockSpec(memory_space=pltpu.VMEM),
        scratch_shapes=[
            pltpu.VMEM((ns, nx, ny, nz), F32),
            pltpu.SemaphoreType.DMA((ns, parts)),
        ],
        compiler_params=pltpu.CompilerParams(vmem_limit_bytes=40 << 20),
        name="pack",
    )(field)


def gram(fibres):
    nb, ns, ny, nx, nz = fibres.shape
    order = nb * nx

    def kernel(in_ref, out_ref, terms_ref, held, total, sems):
        def leaving(s):
            return pltpu.make_async_copy(held.at[:, s], terms_ref.at[:, s], sems.at[s])

        total[...] = jnp.zeros_like(total)

        def halve(s):
            for y in range(ny):
                held[0, s, y], held[1, s, y] = split(in_ref[:, s, y].reshape(order, nz))
            leaving(s).start()

        halve(0)
        for s in range(ns):
            if s + 1 < ns:
                halve(s + 1)
            high = jnp.concatenate([held[0, s, y] for y in range(ny)], axis=1)
            low = jnp.concatenate([held[1, s, y] for y in range(ny)], axis=1)
            total[0] += lax.dot_general(high, high, ROWS_BY_ROWS, preferred_element_type=F32)
            total[1] += lax.dot_general(high, low, ROWS_BY_ROWS, preferred_element_type=F32)
        whole = total[0] + (total[1] + total[1].T)
        for h in range(order // LANES):
            out_ref[h * order : (h + 1) * order] = whole[:, h * LANES : (h + 1) * LANES]
        for s in range(ns):
            leaving(s).wait()

    return pl.pallas_call(
        kernel,
        out_shape=(
            jax.ShapeDtypeStruct((order * (order // LANES), LANES), F32),
            pltpu.HBM((2, ns, ny, order, nz), BF16),
        ),
        in_specs=[pl.BlockSpec(memory_space=pltpu.VMEM)],
        out_specs=(pl.BlockSpec(memory_space=pltpu.VMEM), pl.BlockSpec(memory_space=pl.ANY)),
        scratch_shapes=[
            pltpu.VMEM((2, ns, ny, order, nz), BF16),
            pltpu.VMEM((2, order, order), F32),
            pltpu.SemaphoreType.DMA((ns,)),
        ],
        compiler_params=pltpu.CompilerParams(vmem_limit_bytes=30 << 20),
        name="gram",
    )(fibres)


def sum_everywhere(partial):
    n, m = partial.shape
    everyone = ("yz", "sp")
    size = lax.axis_size("yz") * lax.axis_size("sp")
    parts = lax.all_to_all(partial.reshape(size, n // size, m), everyone, 0, 0, tiled=True)
    copies = jnp.broadcast_to(jnp.sum(parts, axis=0)[None], parts.shape)
    return lax.all_to_all(copies, everyone, 0, 0, tiled=True).reshape(n, m)


def eliminate(square, rows, put, size=8):
    count, width = rows.shape
    halves = width // LANES
    spread = lambda value: jnp.broadcast_to(value, (size, LANES))
    left = [
        [square[t : t + size]] + [rows[t : t + size, h * LANES : (h + 1) * LANES] for h in range(halves)]
        for t in range(0, count, size)
    ]
    for block in range(count // size):
        first = block * size
        rest = range(block + 1, count // size)
        pivots = [[spread(part[i : i + 1]) for part in left[block]] for i in range(size)]
        entry = [
            [spread(pivots[i][0][:, first + j : first + j + 1]) for j in range(i + 1)] for i in range(size)
        ]
        columns = [{t: spread(left[t][0][:, first + j : first + j + 1]) for t in rest} for j in range(size)]
        factor = [[None] * size for _ in range(size)]
        inverse = [None] * size
        for j in range(size):
            inverse[j] = 1.0 / entry[j][j]
            for i in range(j + 1, size):
                factor[i][j] = entry[i][j] * inverse[j]
            for i in range(j + 1, size):
                for m in range(j + 1, i + 1):
                    entry[i][m] = entry[i][m] - factor[i][j] * entry[m][j]
        for i in range(size):
            for j in range(i):
                pivots[i] = [a - factor[i][j] * b for a, b in zip(pivots[i], pivots[j])]
                for t in rest:
                    columns[i][t] = columns[i][t] - factor[i][j] * columns[j][t]
            scale = lax.rsqrt(entry[i][i])
            for h in range(halves):
                put(first + i, h, (pivots[i][1 + h] * scale)[0:1])
        for t in rest:
            for i in range(size):
                multiple = columns[i][t] * inverse[i]
                left[t] = [a - multiple * b for a, b in zip(left[t], pivots[i])]


def finish(gram_matrix, start_rows, terms):
    count, order = start_rows.shape
    _, ns, ny, _, nz = terms.shape

    def kernel(gram_ref, start_ref, terms_ref, core_ref, factor_ref, held, made, in_sems, out_sems):
        def arrival(s):
            return pltpu.make_async_copy(terms_ref.at[:, s], held.at[:, s], in_sems.at[s])

        def leaving(s):
            return pltpu.make_async_copy(made.at[s], core_ref.at[s], out_sems.at[s])

        for s in range(ns):
            arrival(s).start()

        def orth(rows, out_ref):
            rows = rows * lax.rsqrt(jnp.sum(rows * rows, axis=1, keepdims=True))
            square = lax.dot_general(rows, rows, ROWS_BY_ROWS, precision=HIGH, preferred_element_type=F32)
            square = jnp.concatenate([square, jnp.zeros((count, LANES - count), F32)], axis=1)

            def put(i, h, value):
                out_ref[i : i + 1, h * LANES : (h + 1) * LANES] = value

            eliminate(square, rows, put)

        whole = jnp.concatenate([gram_ref[h * order : (h + 1) * order] for h in range(order // LANES)], axis=1)
        factor_ref[...] = start_ref[...]

        def step(index, carry):
            orth(jnp.dot(factor_ref[...], whole, precision=HIGH, preferred_element_type=F32), factor_ref)
            return carry

        lax.fori_loop(0, 2, step, 0)

        high_rows, low_rows = split(factor_ref[...])
        both = jnp.concatenate([high_rows, low_rows], axis=0)

        def species(s, carry):
            arrival(s).wait()
            results = []
            for y in range(ny):
                main = jnp.dot(both, held[0, s, y], preferred_element_type=F32)
                more = jnp.dot(high_rows, held[1, s, y], preferred_element_type=F32)
                results.append(main[:count] + (main[count:] + more))
            made[s] = jnp.swapaxes(jnp.stack(results), 0, 1)
            leaving(s).start()
            return carry

        lax.fori_loop(0, ns, species, 0)
        for s in range(ns):
            leaving(s).wait()

    whole_vmem = pl.BlockSpec(memory_space=pltpu.VMEM)
    anywhere = pl.BlockSpec(memory_space=pl.ANY)
    return pl.pallas_call(
        kernel,
        out_shape=(
            jax.ShapeDtypeStruct((ns, count, ny, nz), F32),
            jax.ShapeDtypeStruct((count, order), F32),
        ),
        in_specs=[whole_vmem, whole_vmem, anywhere],
        out_specs=(anywhere, whole_vmem),
        scratch_shapes=[
            pltpu.VMEM((2, ns, ny, order, nz), BF16),
            pltpu.VMEM((ns, count, ny, nz), F32),
            pltpu.SemaphoreType.DMA((ns,)),
            pltpu.SemaphoreType.DMA((ns,)),
        ],
        compiler_params=pltpu.CompilerParams(vmem_limit_bytes=56 << 20),
        name="finish",
    )(gram_matrix, start_rows, terms)


def local(field, start):
    nb = lax.axis_size("yz")
    blocks = pack(field, field.shape[2] // nb)
    fibres = lax.all_to_all(blocks, "yz", split_axis=0, concat_axis=0, tiled=True)
    partial, terms = gram(fibres)
    total = sum_everywhere(partial)
    core_block, factor_rows = finish(total, start.T, terms)
    return (core_block, factor_rows.T)


def solution(mesh):
    in_specs = (P("sp", "yz", None, None), P())
    out_specs = (P("sp", None, "yz", None), P())
    return jax.shard_map(local, mesh=mesh, in_specs=in_specs, out_specs=out_specs, check_vma=False)
```
